32 devices in a mesh: head: 4 (over y, core), ctx: 8 (over z, x).
Axes of the slice: x: 2, y: 2, z: 4, core: 2. Of those that a mesh axis runs over, the one named last changes fastest.
Arguments:
- queries: bfloat16 [6144, 8192], P(('ctx', 'head')), may hold values from -6 to 6
- keys: bfloat16 [6144, 8192], P(('ctx', 'head')), may hold values from -6 to 6
- values: bfloat16 [6144, 8192], P(('ctx', 'head')), may hold values from -6 to 6
- pattern: int32 [3, 8, 6, 6], P(None, 'ctx'), may hold values 0 or 1
Outputs:
- attended: bfloat16 [6144, 8192], P(('ctx', 'head'))
The draws below stay inside these ranges and needn't reach their ends.
All inputs are finite; a program needn't handle non-finite values. No bound on the sum of `pattern` on one device may be relied on, other than what follows from the above.
Results may differ from the reference program's by a relative error of at most 0.009.
Values may be sent and summed in bfloat16 or wider, within the bound.
A program may use at most 192 MiB of HBM per device.

```python
import jax
import jax.numpy as jnp
from jax import lax

H = 64
HD = 128
BLOCK = 128
C = 768
QB = 6
WIDTH = 8192
TOKENS = 6144
N_CTX = 8


def query_key_pair(key):
    base = jax.random.fold_in(key, 7)
    first_key, second_key = jax.random.split(base, 2)
    shape = (TOKENS, H * HD)
    query_draw = jnp.clip(jax.random.normal(first_key, shape, jnp.float32), -6.0, 6.0)
    key_draw = jnp.clip(jax.random.normal(second_key, shape, jnp.float32), -6.0, 6.0)
    return (query_draw, key_draw)


def draw_queries(key, part):
    return query_key_pair(key)[0].astype(jnp.bfloat16)


def draw_keys(key, part):
    return query_key_pair(key)[1].astype(jnp.bfloat16)


def plant(values, rng, smallest, largest):
    extent = values.shape
    spot = [jax.random.randint(jax.random.fold_in(rng, axis), (), 0, extent[axis]) for axis in range(len(extent))]
    values = values.at[tuple(spot)].set(smallest)
    longest = extent.index(max(extent))
    spot[longest] = (spot[longest] + 1) % extent[longest]
    return values.at[tuple(spot)].set(largest)


def levels(rng, shape, pieces, low, largest):
    def one(dim, parts):
        draws = jax.random.uniform(jax.random.fold_in(jax.random.fold_in(rng, 6), dim), (parts,), jnp.float32, low / len(pieces), largest / len(pieces))
        return jnp.repeat(jnp.exp(draws), shape[dim] // parts).reshape((-1,) + (1,) * (len(shape) - dim - 1))

    level = one(*pieces[0])
    for cut in pieces[1:]:
        level = level * one(*cut)
    return level


def bell_draw(stream_key, dims, spread, limit, pieces=(), kind=jnp.bfloat16):
    loudness = levels(stream_key, dims, pieces, -0.22, 0.18) if pieces else 1.0
    values = jax.random.normal(stream_key, dims, jnp.float32) * spread * loudness
    return jnp.minimum(jnp.maximum(values, -limit), limit).astype(kind)


def setup_inputs(seed: int = 0) -> dict:
    seeds = jax.random.split(jax.random.key(seed), 5)
    queries = draw_queries(jax.random.fold_in(seeds[4], 71), 0)
    keys = draw_keys(jax.random.fold_in(seeds[4], 71), 0)
    values = bell_draw(seeds[2], (TOKENS, WIDTH), 1.0, 6.0, ((0, 32),))
    pattern = plant((jax.random.randint(seeds[3], (3, N_CTX, QB, QB), 0, 2) < 1).astype(jnp.int32), jax.random.fold_in(seeds[3], 1), 0, 1)
    return {"queries": queries, "keys": keys, "values": values, "pattern": pattern}


masked_score = -1e30


def block_allow(block_flags):
    tiled = jnp.broadcast_to(block_flags[:, None, :, None], (QB, BLOCK, QB, BLOCK))
    return tiled.reshape(QB * BLOCK, QB * BLOCK) > 0


def reference(queries, keys, values, pattern):
    far = N_CTX // 2
    distances = (far - 1, far, far + 1)
    scaling = HD ** -0.5
    tok_rows = jnp.arange(C, dtype=jnp.int32)
    causal = tok_rows[:, None] >= tok_rows[None, :]

    def take_rows(array, first_row):
        return lax.dynamic_slice_in_dim(array, first_row, C, 0)

    def one_span(span):
        first_row = (span * C).astype(jnp.int32)
        key_parts = [take_rows(keys, first_row)]
        value_parts = [take_rows(values, first_row)]
        allow_parts = [causal]
        for number, distance in enumerate(distances):
            source_row = (jnp.maximum(span - distance, 0) * C).astype(jnp.int32)
            key_parts.append(take_rows(keys, source_row))
            value_parts.append(take_rows(values, source_row))
            block_flags = lax.dynamic_index_in_dim(pattern[number], span, 0, keepdims=False)
            allow_parts.append(block_allow(block_flags) & (span >= distance))
        key_all = jnp.concatenate(key_parts, 0)
        value_all = jnp.concatenate(value_parts, 0)
        allowed = jnp.concatenate(allow_parts, 1)
        span_queries = take_rows(queries, first_row)

        def one_head(head):
            column = (head * HD).astype(jnp.int32)
            head_queries = lax.dynamic_slice_in_dim(span_queries, column, HD, 1)
            head_keys = lax.dynamic_slice_in_dim(key_all, column, HD, 1)
            head_values = lax.dynamic_slice_in_dim(value_all, column, HD, 1)
            scores = jnp.dot(head_queries, head_keys.T, preferred_element_type=jnp.float32) * scaling
            scores = jnp.where(allowed, scores, masked_score)
            maxima = jnp.max(scores, axis=1, keepdims=True)
            expo = jnp.where(allowed, jnp.exp(scores - maxima), 0.0)
            weights = (expo / jnp.sum(expo, axis=1, keepdims=True)).astype(jnp.bfloat16)
            return jnp.dot(weights, head_values, preferred_element_type=jnp.float32).astype(jnp.bfloat16)

        per_head = lax.map(one_head, jnp.arange(H, dtype=jnp.int32))
        return per_head.transpose(1, 0, 2).reshape(C, H * HD)

    result = lax.map(one_span, jnp.arange(N_CTX, dtype=jnp.int32))
    return result.reshape(TOKENS, H * HD)
```

```python
import functools

import jax
import jax.numpy as jnp
from jax import lax
from jax.experimental import pallas as pl
from jax.experimental.pallas import tpu as pltpu
from jax.sharding import PartitionSpec as P

HD = 128
BLOCK = 128
CHUNKS = 4
LOG2E = 1.4426950408889634
MASKED = -1e30


def tile_rows(total):
    return 2 * BLOCK if total % (2 * BLOCK) == 0 else BLOCK


def as_row(column):
    return jnp.transpose(jnp.broadcast_to(column, (BLOCK, BLOCK)))[0:1, :]


def as_rows(row):
    return jnp.transpose(jnp.broadcast_to(row, (BLOCK, BLOCK)))


def far_kernel(slots, scale, flags_ref, q_ref, *refs):
    kv_refs = refs[: 2 * slots]
    out_ref, lse_ref = refs[2 * slots :]
    rows = q_ref.shape[0]
    blocks = rows // BLOCK
    tile = tile_rows(rows)
    sub = tile // BLOCK
    live = flags_ref[slots * blocks * blocks] > 0

    @pl.when(live)
    def _():
        def step(index, carry):
            start = pl.multiple_of(index * tile, tile)
            q = q_ref[pl.ds(start, tile), :]
            parts = []
            for slot in range(slots):
                s = lax.dot_general(
                    q, kv_refs[2 * slot][...], (((1,), (1,)), ((), ())),
                    preferred_element_type=jnp.float32,
                )
                lines = []
                for r in range(sub):
                    cells = []
                    for b in range(blocks):
                        flag = flags_ref[(slot * blocks + index * sub + r) * blocks + b]
                        bias = jnp.where(flag > 0, 0.0, MASKED)
                        cells.append(
                            s[r * BLOCK : (r + 1) * BLOCK, b * BLOCK : (b + 1) * BLOCK] * scale + bias
                        )
                    lines.append(jnp.concatenate(cells, axis=1))
                parts.append(jnp.concatenate(lines, axis=0) if sub > 1 else lines[0])
            top = functools.reduce(jnp.maximum, [jnp.max(p, axis=1, keepdims=True) for p in parts])
            total = jnp.zeros((tile, 1), jnp.float32)
            mix = jnp.zeros((tile, HD), jnp.float32)
            for slot in range(slots):
                e = jnp.exp2(parts[slot] - top)
                total += jnp.sum(e, axis=1, keepdims=True)
                mix += jnp.dot(
                    e.astype(jnp.bfloat16), kv_refs[2 * slot + 1][...],
                    preferred_element_type=jnp.float32,
                )
            out_ref[pl.ds(start, tile), :] = (mix / total).astype(jnp.bfloat16)
            lse = top + jnp.log2(total)
            for r in range(sub):
                lse_ref[0, :, pl.ds(pl.multiple_of(start + r * BLOCK, BLOCK), BLOCK)] = as_row(
                    lse[r * BLOCK : (r + 1) * BLOCK]
                )
            return carry

        lax.fori_loop(0, rows // tile, step, 0)

    @pl.when(jnp.logical_not(live))
    def _():
        out_ref[...] = jnp.zeros_like(out_ref)
        lse_ref[...] = jnp.full_like(lse_ref, MASKED)


def far_attention(flags, q, kvs):
    rows, width = q.shape
    heads = width // HD
    slots = len(kvs)
    scale = HD ** -0.5 * LOG2E
    live = jnp.max(flags).reshape(1)
    flat = jnp.concatenate([flags.reshape(-1), live])
    here = pl.BlockSpec((rows, HD), lambda h: (0, h))
    there = pl.BlockSpec((rows, HD), lambda h: (0, h + heads))
    operands = []
    for kv in kvs:
        operands += [kv, kv]
    return pl.pallas_call(
        functools.partial(far_kernel, slots, scale),
        grid=(heads,),
        in_specs=[pl.BlockSpec(memory_space=pltpu.SMEM), here] + [here, there] * slots,
        out_specs=[here, pl.BlockSpec((1, 1, rows), lambda h: (h, 0, 0))],
        out_shape=[
            jax.ShapeDtypeStruct((rows, width), jnp.bfloat16),
            jax.ShapeDtypeStruct((heads, 1, rows), jnp.float32),
        ],
        cost_estimate=pl.CostEstimate(
            flops=4 * slots * rows * rows * width,
            bytes_accessed=2 * rows * width * (2 + 2 * slots),
            transcendentals=slots * rows * rows * heads,
        ),
        compiler_params=pltpu.CompilerParams(vmem_limit_bytes=40 << 20),
    )(flat, q, *operands)


def near_kernel(scale, q_ref, k_ref, v_ref, far_ref, odd_ref, far_lse_ref, odd_lse_ref, out_ref):
    rows = q_ref.shape[0]
    tile = tile_rows(rows)
    below = (
        lax.broadcasted_iota(jnp.int32, (tile, tile), 0)
        >= lax.broadcasted_iota(jnp.int32, (tile, tile), 1)
    )
    for index in range(rows // tile):
        start = index * tile
        end = start + tile
        q = q_ref[start:end, :]
        s = lax.dot_general(
            q, k_ref[0:end, :], (((1,), (1,)), ((), ())), preferred_element_type=jnp.float32
        ) * scale
        corner = jnp.where(below, s[:, start:end], MASKED)
        s = jnp.concatenate([s[:, :start], corner], axis=1) if index else corner
        top = jnp.max(s, axis=1, keepdims=True)
        e = jnp.exp2(s - top)
        total = jnp.sum(e, axis=1, keepdims=True)
        mix = jnp.dot(
            e.astype(jnp.bfloat16), v_ref[0:end, :], preferred_element_type=jnp.float32
        )
        for r in range(start, end, BLOCK):
            part = slice(r - start, r - start + BLOCK)
            far = as_rows(far_lse_ref[0, :, r : r + BLOCK])
            odd = as_rows(odd_lse_ref[0, :, r : r + BLOCK])
            best = jnp.maximum(jnp.maximum(far, odd), top[part])
            own_w = jnp.exp2(top[part] - best)
            far_w = jnp.exp2(far - best)
            odd_w = jnp.exp2(odd - best)
            numerator = (
                mix[part] * own_w
                + far_ref[r : r + BLOCK, :].astype(jnp.float32) * far_w
                + odd_ref[r : r + BLOCK, :].astype(jnp.float32) * odd_w
            )
            out_ref[r : r + BLOCK, :] = (
                numerator / (total[part] * own_w + far_w + odd_w)
            ).astype(jnp.bfloat16)


def near_attention(q, kv, far, far_lse, odd, odd_lse):
    rows, width = q.shape
    heads = width // HD
    scale = HD ** -0.5 * LOG2E
    here = pl.BlockSpec((rows, HD), lambda h: (0, h))
    there = pl.BlockSpec((rows, HD), lambda h: (0, h + heads))
    line = pl.BlockSpec((1, 1, rows), lambda h: (h, 0, 0))
    return pl.pallas_call(
        functools.partial(near_kernel, scale),
        grid=(heads,),
        in_specs=[here, here, there, here, here, line, line],
        out_specs=here,
        out_shape=jax.ShapeDtypeStruct((rows, width), jnp.bfloat16),
        cost_estimate=pl.CostEstimate(
            flops=2 * rows * rows * width,
            bytes_accessed=2 * rows * width * 6,
            transcendentals=rows * rows * heads // 2,
        ),
        compiler_params=pltpu.CompilerParams(vmem_limit_bytes=40 << 20),
    )(q, kv, kv, far, odd, far_lse, odd_lse)


def body(queries, keys, values, pattern):
    groups = lax.axis_size("head")
    spans = lax.axis_size("ctx")
    position = lax.axis_index("ctx")
    far = spans // 2
    tok_rows, width = queries.shape
    rows = tok_rows * groups
    group_width = width // groups
    w = group_width // CHUNKS

    to_low = [(q, q - far) for q in range(far, spans)]
    to_high = [(b, a) for a, b in to_low]
    odd_low = [(far - 1, 0), (spans - 1, far)]
    odd_high = [(b, a) for a, b in odd_low]
    swap = [(c, c ^ 1) for c in range(far)]
    relay = [(c, c + 2) for c in range(0, far - 2, 2)] + [(c, c - 2) for c in range(3, far, 2)]

    move = lambda value, pairs: lax.ppermute(value, "ctx", pairs)

    own_flags = pattern[:, 0]
    low_flags = move(own_flags, to_low)
    odd_flags = move(own_flags[:1], odd_low)
    after = jnp.where(position == far - 1, 0, low_flags[0])
    before = jnp.where(position == 0, 0, low_flags[2])
    even = position % 2 == 0
    slot_flags = jnp.stack(
        [low_flags[1], jnp.where(even, after, before), jnp.where(even, before, after)]
    )
    has_far = position >= far
    has_odd = (position == far - 1) | (position == spans - 1)

    def grouped(array, chunk):
        return array.reshape(tok_rows, groups, CHUNKS, w)[:, :, chunk].transpose(1, 0, 2)

    def regroup(array):
        return lax.all_to_all(array, "head", split_axis=0, concat_axis=0, tiled=True)

    results = []
    for chunk in range(CHUNKS):
        kv = regroup(
            jnp.concatenate([grouped(keys, chunk), grouped(values, chunk)], axis=2)
        ).reshape(rows, 2 * w)
        q = regroup(grouped(queries, chunk)).reshape(rows, w)
        q_low = move(q, to_low)
        q_odd = move(q, odd_low)
        kv_pair = move(kv, swap)
        kv_next = move(kv_pair, relay)
        odd_out, odd_lse = far_attention(odd_flags, q_odd, [kv])
        far_out, far_lse = far_attention(slot_flags, q_low, [kv, kv_pair, kv_next])
        far_out, far_lse = move(far_out, to_high), move(far_lse, to_high)
        odd_out, odd_lse = move(odd_out, odd_high), move(odd_lse, odd_high)
        far_lse = jnp.where(has_far, far_lse, MASKED)
        odd_lse = jnp.where(has_odd, odd_lse, MASKED)
        mixed = near_attention(q, kv, far_out, far_lse, odd_out, odd_lse)
        results.append(regroup(mixed.reshape(groups, tok_rows, w)))
    whole = jnp.stack(results, axis=2)
    return whole.transpose(1, 0, 2, 3).reshape(tok_rows, width)


def solution(mesh):
    rows = P(("ctx", "head"), None)
    return jax.shard_map(
        body,
        mesh=mesh,
        in_specs=(rows, rows, rows, P(None, "ctx", None, None)),
        out_specs=rows,
        check_vma=False,
    )
```

```python
import functools

import jax
import jax.numpy as jnp
from jax import lax
from jax.experimental import pallas as pl
from jax.experimental.pallas import tpu as pltpu
from jax.sharding import PartitionSpec as P

HD = 128
BLOCK = 128
CHUNKS = 4
LOG2E = 1.4426950408889634
MASKED = -1e30


def tile_rows(total):
    return 2 * BLOCK if total % (2 * BLOCK) == 0 else BLOCK


def as_row(column):
    return jnp.transpose(jnp.broadcast_to(column, (BLOCK, BLOCK)))[0:1, :]


def as_rows(row):
    return jnp.transpose(jnp.broadcast_to(row, (BLOCK, BLOCK)))


def far_kernel(slots, scale, flags_ref, q_ref, *refs):
    kv_refs = refs[: 2 * slots]
    out_ref, lse_ref = refs[2 * slots :]
    rows = q_ref.shape[0]
    blocks = rows // BLOCK
    tile = tile_rows(rows)
    sub = tile // BLOCK
    live = flags_ref[slots * blocks * blocks] > 0

    @pl.when(live)
    def _():
        def step(index, carry):
            start = pl.multiple_of(index * tile, tile)
            q = q_ref[pl.ds(start, tile), :]
            parts = []
            for slot in range(slots):
                s = lax.dot_general(
                    q, kv_refs[2 * slot][...], (((1,), (1,)), ((), ())),
                    preferred_element_type=jnp.float32,
                )
                lines = []
                for r in range(sub):
                    cells = []
                    for b in range(blocks):
                        flag = flags_ref[(slot * blocks + index * sub + r) * blocks + b]
                        bias = jnp.where(flag > 0, 0.0, MASKED)
                        cells.append(
                            s[r * BLOCK : (r + 1) * BLOCK, b * BLOCK : (b + 1) * BLOCK] * scale + bias
                        )
                    lines.append(jnp.concatenate(cells, axis=1))
                parts.append(jnp.concatenate(lines, axis=0) if sub > 1 else lines[0])
            top = functools.reduce(jnp.maximum, [jnp.max(p, axis=1, keepdims=True) for p in parts])
            total = jnp.zeros((tile, 1), jnp.float32)
            mix = jnp.zeros((tile, HD), jnp.float32)
            for slot in range(slots):
                e = jnp.exp2(parts[slot] - top)
                total += jnp.sum(e, axis=1, keepdims=True)
                mix += jnp.dot(
                    e.astype(jnp.bfloat16), kv_refs[2 * slot + 1][...],
                    preferred_element_type=jnp.float32,
                )
            out_ref[pl.ds(start, tile), :] = (mix / total).astype(jnp.bfloat16)
            lse = top + jnp.log2(total)
            for r in range(sub):
                lse_ref[0, :, pl.ds(pl.multiple_of(start + r * BLOCK, BLOCK), BLOCK)] = as_row(
                    lse[r * BLOCK : (r + 1) * BLOCK]
                )
            return carry

        lax.fori_loop(0, rows // tile, step, 0)

    @pl.when(jnp.logical_not(live))
    def _():
        out_ref[...] = jnp.zeros_like(out_ref)
        lse_ref[...] = jnp.full_like(lse_ref, MASKED)


def far_attention(flags, q, kvs):
    rows, width = q.shape
    heads = width // HD
    slots = len(kvs)
    scale = HD ** -0.5 * LOG2E
    live = jnp.max(flags).reshape(1)
    flat = jnp.concatenate([flags.reshape(-1), live])
    here = pl.BlockSpec((rows, HD), lambda h: (0, h))
    there = pl.BlockSpec((rows, HD), lambda h: (0, h + heads))
    operands = []
    for kv in kvs:
        operands += [kv, kv]
    return pl.pallas_call(
        functools.partial(far_kernel, slots, scale),
        grid=(heads,),
        in_specs=[pl.BlockSpec(memory_space=pltpu.SMEM), here] + [here, there] * slots,
        out_specs=[here, pl.BlockSpec((1, 1, rows), lambda h: (h, 0, 0))],
        out_shape=[
            jax.ShapeDtypeStruct((rows, width), jnp.bfloat16),
            jax.ShapeDtypeStruct((heads, 1, rows), jnp.float32),
        ],
        cost_estimate=pl.CostEstimate(
            flops=4 * slots * rows * rows * width,
            bytes_accessed=2 * rows * width * (2 + 2 * slots),
            transcendentals=slots * rows * rows * heads,
        ),
        compiler_params=pltpu.CompilerParams(vmem_limit_bytes=40 << 20),
    )(flat, q, *operands)


def near_kernel(scale, q_ref, k_ref, v_ref, far_ref, odd_ref, far_lse_ref, odd_lse_ref, out_ref):
    rows = q_ref.shape[0]
    tile = tile_rows(rows)
    below = (
        lax.broadcasted_iota(jnp.int32, (tile, tile), 0)
        >= lax.broadcasted_iota(jnp.int32, (tile, tile), 1)
    )
    for index in range(rows // tile):
        start = index * tile
        end = start + tile
        q = q_ref[start:end, :]
        s = lax.dot_general(
            q, k_ref[0:end, :], (((1,), (1,)), ((), ())), preferred_element_type=jnp.float32
        ) * scale
        corner = jnp.where(below, s[:, start:end], MASKED)
        s = jnp.concatenate([s[:, :start], corner], axis=1) if index else corner
        top = jnp.max(s, axis=1, keepdims=True)
        e = jnp.exp2(s - top)
        total = jnp.sum(e, axis=1, keepdims=True)
        mix = jnp.dot(
            e.astype(jnp.bfloat16), v_ref[0:end, :], preferred_element_type=jnp.float32
        )
        for r in range(start, end, BLOCK):
            part = slice(r - start, r - start + BLOCK)
            far = as_rows(far_lse_ref[0, :, r : r + BLOCK])
            odd = as_rows(odd_lse_ref[0, :, r : r + BLOCK])
            best = jnp.maximum(jnp.maximum(far, odd), top[part])
            own_w = jnp.exp2(top[part] - best)
            far_w = jnp.exp2(far - best)
            odd_w = jnp.exp2(odd - best)
            numerator = (
                mix[part] * own_w
                + far_ref[r : r + BLOCK, :].astype(jnp.float32) * far_w
                + odd_ref[r : r + BLOCK, :].astype(jnp.float32) * odd_w
            )
            out_ref[r : r + BLOCK, :] = (
                numerator / (total[part] * own_w + far_w + odd_w)
            ).astype(jnp.bfloat16)


def near_attention(q, kv, far, far_lse, odd, odd_lse):
    rows, width = q.shape
    heads = width // HD
    scale = HD ** -0.5 * LOG2E
    here = pl.BlockSpec((rows, HD), lambda h: (0, h))
    there = pl.BlockSpec((rows, HD), lambda h: (0, h + heads))
    line = pl.BlockSpec((1, 1, rows), lambda h: (h, 0, 0))
    return pl.pallas_call(
        functools.partial(near_kernel, scale),
        grid=(heads,),
        in_specs=[here, here, there, here, here, line, line],
        out_specs=here,
        out_shape=jax.ShapeDtypeStruct((rows, width), jnp.bfloat16),
        cost_estimate=pl.CostEstimate(
            flops=2 * rows * rows * width,
            bytes_accessed=2 * rows * width * 6,
            transcendentals=rows * rows * heads // 2,
        ),
        compiler_params=pltpu.CompilerParams(vmem_limit_bytes=40 << 20),
    )(q, kv, kv, far, odd, far_lse, odd_lse)


def body(queries, keys, values, pattern):
    groups = lax.axis_size("head")
    spans = lax.axis_size("ctx")
    position = lax.axis_index("ctx")
    far = spans // 2
    tok_rows, width = queries.shape
    rows = tok_rows * groups
    group_width = width // groups
    w = group_width // CHUNKS

    to_low = [(q, q - far) for q in range(far, spans)]
    to_high = [(b, a) for a, b in to_low]
    odd_low = [(far - 1, 0), (spans - 1, far)]
    odd_high = [(b, a) for a, b in odd_low]
    swap = [(c, c ^ 1) for c in range(far)]
    relay = [(c, c + 2) for c in range(0, far - 2, 2)] + [(c, c - 2) for c in range(3, far, 2)]

    move = lambda value, pairs: lax.ppermute(value, "ctx", pairs)

    own_flags = pattern[:, 0]
    low_flags = move(own_flags, to_low)
    odd_flags = move(own_flags[:1], odd_low)
    after = jnp.where(position == far - 1, 0, low_flags[0])
    before = jnp.where(position == 0, 0, low_flags[2])
    even = position % 2 == 0
    slot_flags = jnp.stack(
        [low_flags[1], jnp.where(even, after, before), jnp.where(even, before, after)]
    )
    has_far = position >= far
    has_odd = (position == far - 1) | (position == spans - 1)

    def grouped(array, chunk):
        return array.reshape(tok_rows, groups, CHUNKS, w)[:, :, chunk].transpose(1, 0, 2)

    def regroup(array):
        return lax.all_to_all(array, "head", split_axis=0, concat_axis=0, tiled=True)

    def gather(chunk, state):
        kv = regroup(
            jnp.concatenate(
                [grouped(state["keys"], chunk), grouped(state["values"], chunk)], axis=2
            )
        ).reshape(rows, 2 * w)
        q = regroup(grouped(state["queries"], chunk)).reshape(rows, w)
        return {"kv": kv, "q": q}

    def spread(item):
        return {
            **item,
            "q_low": move(item["q"], to_low),
            "q_odd": move(item["q"], odd_low),
            "kv_pair": move(item["kv"], swap),
        }

    def pass_on(item):
        odd_out, odd_lse = far_attention(state["odd_flags"], item["q_odd"], [item["kv"]])
        return {
            **item,
            "kv_next": move(item["kv_pair"], relay),
            "odd_out": odd_out,
            "odd_lse": odd_lse,
        }

    def attend(item):
        out, lse = far_attention(
            state["slot_flags"], item["q_low"], [item["kv"], item["kv_pair"], item["kv_next"]]
        )
        return {
            "q": item["q"],
            "kv": item["kv"],
            "far_out": out,
            "far_lse": lse,
            "odd_out": move(item["odd_out"], odd_high),
            "odd_lse": move(item["odd_lse"], odd_high),
        }

    def give_back(item):
        return {
            **item,
            "far_out": move(item["far_out"], to_high),
            "far_lse": move(item["far_lse"], to_high),
        }

    def finish(item):
        far_lse = jnp.where(has_far, item["far_lse"], MASKED)
        odd_lse = jnp.where(has_odd, item["odd_lse"], MASKED)
        mixed = near_attention(
            item["q"], item["kv"], item["far_out"], far_lse, item["odd_out"], odd_lse
        )
        return {"done": regroup(mixed.reshape(groups, tok_rows, w))}

    stages = (spread, pass_on, attend, give_back, finish)
    state = {
        "queries": queries,
        "keys": keys,
        "values": values,
        "slot_flags": slot_flags,
        "odd_flags": odd_flags,
    }
    state = lax.optimization_barrier(state)
    items = {}
    for step in range(CHUNKS + len(stages)):
        ahead = {}
        for chunk in range(CHUNKS):
            stage = step - chunk
            if stage == 0:
                ahead[chunk] = gather(chunk, state)
            elif 0 < stage <= len(stages):
                ahead[chunk] = stages[stage - 1](items[chunk])
            elif chunk in items:
                ahead[chunk] = items[chunk]
        items, state = lax.optimization_barrier((ahead, state))
    results = [items[chunk]["done"] for chunk in range(CHUNKS)]
    whole = jnp.stack(results, axis=2)
    return whole.transpose(1, 0, 2, 3).reshape(tok_rows, width)


def solution(mesh):
    rows = P(("ctx", "head"), None)
    return jax.shard_map(
        body,
        mesh=mesh,
        in_specs=(rows, rows, rows, P(None, "ctx", None, None)),
        out_specs=rows,
        check_vma=False,
    )
```

```python
import functools

import jax
import jax.numpy as jnp
from jax import lax
from jax.experimental import pallas as pl
from jax.experimental.pallas import tpu as pltpu
from jax.sharding import PartitionSpec as P

HD = 128
BLOCK = 128
CHUNKS = 4
LOG2E = 1.4426950408889634
MASKED = -1e30


def tile_rows(total):
    return 2 * BLOCK if total % (2 * BLOCK) == 0 else BLOCK


def turned(square):
    return jnp.transpose(square)


def as_rows(row):
    return turned(jnp.broadcast_to(row, (BLOCK, BLOCK)))


def with_ones(values):
    return jnp.concatenate([values, jnp.ones_like(values)], axis=1)


def far_kernel(slots, scale, flags_ref, q_ref, *refs):
    kv_refs = refs[: 2 * slots]
    out_ref, lse_ref = refs[2 * slots :]
    rows = q_ref.shape[0]
    blocks = rows // BLOCK
    tile = tile_rows(rows)
    sub = tile // BLOCK
    live = flags_ref[slots * blocks * blocks] > 0

    @pl.when(live)
    def _():
        wide = [with_ones(kv_refs[2 * slot + 1][...]) for slot in range(slots)]
        for index in range(rows // tile):
            start = index * tile
            q = q_ref[start : start + tile, :]
            parts = []
            for slot in range(slots):
                s = lax.dot_general(
                    q, kv_refs[2 * slot][...], (((1,), (1,)), ((), ())),
                    preferred_element_type=jnp.float32,
                )
                lines = []
                for r in range(sub):
                    cells = []
                    for b in range(blocks):
                        flag = flags_ref[(slot * blocks + index * sub + r) * blocks + b]
                        bias = jnp.where(flag > 0, 0.0, MASKED)
                        cells.append(
                            s[r * BLOCK : (r + 1) * BLOCK, b * BLOCK : (b + 1) * BLOCK] * scale + bias
                        )
                    lines.append(jnp.concatenate(cells, axis=1))
                parts.append(jnp.concatenate(lines, axis=0) if sub > 1 else lines[0])
            top = functools.reduce(jnp.maximum, [jnp.max(p, axis=1, keepdims=True) for p in parts])
            mix = jnp.zeros((tile, 2 * HD), jnp.float32)
            for slot in range(slots):
                e = jnp.exp2(parts[slot] - top).astype(jnp.bfloat16)
                mix += jnp.dot(e, wide[slot], preferred_element_type=jnp.float32)
            total = mix[:, HD:]
            out_ref[start : start + tile, :] = (mix[:, :HD] / total).astype(jnp.bfloat16)
            lse = top + jnp.log2(total)
            for r in range(sub):
                line = index * sub + r
                lse_ref[line : line + 1, :] = turned(lse[r * BLOCK : (r + 1) * BLOCK])[0:1, :]

    @pl.when(jnp.logical_not(live))
    def _():
        out_ref[0:rows, :] = jnp.zeros((rows, HD), out_ref.dtype)
        lse_ref[...] = jnp.full_like(lse_ref, MASKED)

    rest = lse_ref[...]
    pad = lse_ref.shape[0]
    for piece in range(3):
        part = rest.astype(jnp.bfloat16)
        out_ref[rows + piece * pad : rows + (piece + 1) * pad, :] = part
        rest = rest - part.astype(jnp.float32)


def pad_rows(rows):
    return -(-(rows // BLOCK) // 16) * 16


def far_attention(flags, q, kvs):
    rows, width = q.shape
    heads = width // HD
    slots = len(kvs)
    scale = HD ** -0.5 * LOG2E
    tall = rows + 3 * pad_rows(rows)
    live = jnp.max(flags).reshape(1)
    flat = jnp.concatenate([flags.reshape(-1), live])
    here = pl.BlockSpec((rows, HD), lambda h: (0, h))
    there = pl.BlockSpec((rows, HD), lambda h: (0, h + heads))
    operands = []
    for kv in kvs:
        operands += [kv, kv]
    return pl.pallas_call(
        functools.partial(far_kernel, slots, scale),
        grid=(heads,),
        in_specs=[pl.BlockSpec(memory_space=pltpu.SMEM), here] + [here, there] * slots,
        out_specs=pl.BlockSpec((tall, HD), lambda h: (0, h)),
        out_shape=jax.ShapeDtypeStruct((tall, width), jnp.bfloat16),
        scratch_shapes=[pltpu.VMEM((pad_rows(rows), BLOCK), jnp.float32)],
        cost_estimate=pl.CostEstimate(
            flops=4 * slots * rows * rows * width,
            bytes_accessed=2 * rows * width * (2 + 2 * slots),
            transcendentals=slots * rows * rows * heads,
        ),
        compiler_params=pltpu.CompilerParams(vmem_limit_bytes=40 << 20),
    )(flat, q, *operands)


def near_kernel(scale, has_ref, q_ref, k_ref, v_ref, far_ref, odd_ref, out_ref):
    rows = q_ref.shape[0]
    tile = tile_rows(rows)
    pad = pad_rows(rows)

    def log_sums(ref, has):
        pieces = [
            ref[rows + p * pad : rows + (p + 1) * pad, :].astype(jnp.float32) for p in range(3)
        ]
        return jnp.where(has, (pieces[0] + pieces[1]) + pieces[2], MASKED)

    far_all = log_sums(far_ref, has_ref[0] > 0)
    odd_all = log_sums(odd_ref, has_ref[1] > 0)
    wide = with_ones(v_ref[...])
    below = (
        lax.broadcasted_iota(jnp.int32, (tile, tile), 0)
        >= lax.broadcasted_iota(jnp.int32, (tile, tile), 1)
    )
    for index in range(rows // tile):
        start = index * tile
        end = start + tile
        q = q_ref[start:end, :]
        s = lax.dot_general(
            q, k_ref[0:end, :], (((1,), (1,)), ((), ())), preferred_element_type=jnp.float32
        ) * scale
        corner = jnp.where(below, s[:, start:end], MASKED)
        s = jnp.concatenate([s[:, :start], corner], axis=1) if index else corner
        top = jnp.max(s, axis=1, keepdims=True)
        e = jnp.exp2(s - top).astype(jnp.bfloat16)
        mix = jnp.dot(e, wide[0:end, :], preferred_element_type=jnp.float32)
        for r in range(start, end, BLOCK):
            part = slice(r - start, r - start + BLOCK)
            line = r // BLOCK
            far = as_rows(far_all[line : line + 1, :])
            odd = as_rows(odd_all[line : line + 1, :])
            best = jnp.maximum(jnp.maximum(far, odd), top[part])
            own_w = jnp.exp2(top[part] - best)
            far_w = jnp.exp2(far - best)
            odd_w = jnp.exp2(odd - best)
            numerator = (
                mix[part, :HD] * own_w
                + far_ref[r : r + BLOCK, :].astype(jnp.float32) * far_w
                + odd_ref[r : r + BLOCK, :].astype(jnp.float32) * odd_w
            )
            out_ref[r : r + BLOCK, :] = (
                numerator / (mix[part, HD:] * own_w + far_w + odd_w)
            ).astype(jnp.bfloat16)


def near_attention(has, q, kv, far, odd):
    rows, width = q.shape
    heads = width // HD
    scale = HD ** -0.5 * LOG2E
    here = pl.BlockSpec((rows, HD), lambda h: (0, h))
    there = pl.BlockSpec((rows, HD), lambda h: (0, h + heads))
    tall = pl.BlockSpec((far.shape[0], HD), lambda h: (0, h))
    return pl.pallas_call(
        functools.partial(near_kernel, scale),
        grid=(heads,),
        in_specs=[pl.BlockSpec(memory_space=pltpu.SMEM), here, here, there, tall, tall],
        out_specs=here,
        out_shape=jax.ShapeDtypeStruct((rows, width), jnp.bfloat16),
        cost_estimate=pl.CostEstimate(
            flops=2 * rows * rows * width,
            bytes_accessed=2 * rows * width * 6,
            transcendentals=rows * rows * heads // 2,
        ),
        compiler_params=pltpu.CompilerParams(vmem_limit_bytes=40 << 20),
    )(has, q, kv, kv, far, odd)


def body(queries, keys, values, pattern):
    groups = lax.axis_size("head")
    spans = lax.axis_size("ctx")
    position = lax.axis_index("ctx")
    far = spans // 2
    tok_rows, width = queries.shape
    rows = tok_rows * groups
    group_width = width // groups
    w = group_width // CHUNKS

    to_low = [(q, q - far) for q in range(far, spans)]
    to_high = [(b, a) for a, b in to_low]
    odd_low = [(far - 1, 0), (spans - 1, far)]
    odd_high = [(b, a) for a, b in odd_low]
    swap = [(c, c ^ 1) for c in range(far)]
    relay = [(c, c + 2) for c in range(0, far - 2, 2)] + [(c, c - 2) for c in range(3, far, 2)]

    move = lambda value, pairs: lax.ppermute(value, "ctx", pairs)

    own_flags = pattern[:, 0]
    low_flags = move(own_flags, to_low)
    odd_flags = move(own_flags[:1], odd_low)
    after = jnp.where(position == far - 1, 0, low_flags[0])
    before = jnp.where(position == 0, 0, low_flags[2])
    even = position % 2 == 0
    slot_flags = jnp.stack(
        [low_flags[1], jnp.where(even, after, before), jnp.where(even, before, after)]
    )
    has = jnp.stack(
        [position >= far, (position == far - 1) | (position == spans - 1)]
    ).astype(jnp.int32)

    def columns(array, group, chunk):
        first = group * group_width + chunk * w
        return lax.slice_in_dim(array, first, first + w, axis=1)

    def grouped(arrays, chunk):
        return jnp.concatenate(
            [
                jnp.concatenate([columns(array, group, chunk) for array in arrays], axis=1)
                for group in range(groups)
            ],
            axis=0,
        ).reshape(groups, tok_rows, len(arrays) * w)

    def regroup(array):
        return lax.all_to_all(array, "head", split_axis=0, concat_axis=0, tiled=True)

    def gather(chunk, state):
        kv = regroup(grouped([state["keys"], state["values"]], chunk)).reshape(rows, 2 * w)
        q = regroup(grouped([state["queries"]], chunk)).reshape(rows, w)
        return {"kv": kv, "q": q}

    def spread(item):
        return {
            **item,
            "q_low": move(item["q"], to_low),
            "q_odd": move(item["q"], odd_low),
            "kv_pair": move(item["kv"], swap),
        }

    def pass_on(item):
        return {
            **item,
            "kv_next": move(item["kv_pair"], relay),
            "odd_out": far_attention(state["odd_flags"], item["q_odd"], [item["kv"]]),
        }

    def attend(item):
        out = far_attention(
            state["slot_flags"], item["q_low"], [item["kv"], item["kv_pair"], item["kv_next"]]
        )
        return {
            "q": item["q"],
            "kv": item["kv"],
            "far_out": out,
            "odd_out": move(item["odd_out"], odd_high),
        }

    def give_back(item):
        return {
            **item,
            "far_out": move(item["far_out"], to_high),
        }

    def finish(item):
        mixed = near_attention(has, item["q"], item["kv"], item["far_out"], item["odd_out"])
        return {"done": regroup(mixed.reshape(groups, tok_rows, w))}

    stages = (spread, pass_on, attend, give_back, finish)
    state = {
        "queries": queries,
        "keys": keys,
        "values": values,
        "slot_flags": slot_flags,
        "odd_flags": odd_flags,
    }
    state = lax.optimization_barrier(state)
    items = {}
    for step in range(CHUNKS + len(stages)):
        ahead = {}
        for chunk in range(CHUNKS):
            stage = step - chunk
            if stage == 0:
                ahead[chunk] = gather(chunk, state)
            elif 0 < stage <= len(stages):
                ahead[chunk] = stages[stage - 1](items[chunk])
            elif chunk in items:
                ahead[chunk] = items[chunk]
        items, state = lax.optimization_barrier((ahead, state))
    results = [items[chunk]["done"] for chunk in range(CHUNKS)]
    return jnp.concatenate(
        [results[chunk][group] for group in range(groups) for chunk in range(CHUNKS)], axis=1
    )


def solution(mesh):
    rows = P(("ctx", "head"), None)
    return jax.shard_map(
        body,
        mesh=mesh,
        in_specs=(rows, rows, rows, P(None, "ctx", None, None)),
        out_specs=rows,
        check_vma=False,
    )
```

```python
import functools

import jax
import jax.numpy as jnp
from jax import lax
from jax.experimental import pallas as pl
from jax.experimental.pallas import tpu as pltpu
from jax.sharding import PartitionSpec as P

HD = 128
BLOCK = 128
CHUNKS = 4
LOG2E = 1.4426950408889634
MASKED = -1e30


def tile_rows(total):
    return 2 * BLOCK if total % (2 * BLOCK) == 0 else BLOCK


def turned(square):
    return jnp.transpose(square)


def as_rows(row):
    return turned(jnp.broadcast_to(row, (BLOCK, BLOCK)))


def with_ones(values):
    return jnp.concatenate([values, jnp.ones_like(values)], axis=1)


def flat(ref):
    return ref[...].reshape(-1, HD)


def far_kernel(slots, scale, flags_ref, q_ref, *refs):
    kv_refs = refs[: 2 * slots]
    out_ref, lse_ref = refs[2 * slots :]
    rows = q_ref.shape[0]
    blocks = rows // BLOCK
    tile = tile_rows(rows)
    sub = tile // BLOCK
    live = flags_ref[slots * blocks * blocks] > 0

    @pl.when(live)
    def _():
        wide = [with_ones(flat(kv_refs[2 * slot + 1])) for slot in range(slots)]
        heads_keys = [flat(kv_refs[2 * slot]) for slot in range(slots)]
        for index in range(rows // tile):
            start = index * tile
            q = q_ref[start : start + tile, :]
            parts = []
            for slot in range(slots):
                s = lax.dot_general(
                    q, heads_keys[slot], (((1,), (1,)), ((), ())),
                    preferred_element_type=jnp.float32,
                )
                lines = []
                for r in range(sub):
                    cells = []
                    for b in range(blocks):
                        flag = flags_ref[(slot * blocks + index * sub + r) * blocks + b]
                        bias = jnp.where(flag > 0, 0.0, MASKED)
                        cells.append(
                            s[r * BLOCK : (r + 1) * BLOCK, b * BLOCK : (b + 1) * BLOCK] * scale + bias
                        )
                    lines.append(jnp.concatenate(cells, axis=1))
                parts.append(jnp.concatenate(lines, axis=0) if sub > 1 else lines[0])
            top = functools.reduce(jnp.maximum, [jnp.max(p, axis=1, keepdims=True) for p in parts])
            mix = jnp.zeros((tile, 2 * HD), jnp.float32)
            for slot in range(slots):
                e = jnp.exp2(parts[slot] - top).astype(jnp.bfloat16)
                mix += jnp.dot(e, wide[slot], preferred_element_type=jnp.float32)
            total = mix[:, HD:]
            out_ref[start : start + tile, :] = (mix[:, :HD] / total).astype(jnp.bfloat16)
            lse = top + jnp.log2(total)
            for r in range(sub):
                line = index * sub + r
                lse_ref[line : line + 1, :] = turned(lse[r * BLOCK : (r + 1) * BLOCK])[0:1, :]

    @pl.when(jnp.logical_not(live))
    def _():
        out_ref[0:rows, :] = jnp.zeros((rows, HD), out_ref.dtype)
        lse_ref[...] = jnp.full_like(lse_ref, MASKED)

    rest = lse_ref[...]
    pad = lse_ref.shape[0]
    for piece in range(3):
        part = rest.astype(jnp.bfloat16)
        out_ref[rows + piece * pad : rows + (piece + 1) * pad, :] = part
        rest = rest - part.astype(jnp.float32)


def pad_rows(rows):
    return -(-(rows // BLOCK) // 16) * 16


def kv_specs(kv):
    block = (kv.shape[0], 1, kv.shape[2], HD)
    return (
        pl.BlockSpec(block, lambda h: (0, 0, 0, h)),
        pl.BlockSpec(block, lambda h: (0, 1, 0, h)),
    )


def far_attention(flags, q, kvs):
    rows, width = q.shape
    heads = width // HD
    slots = len(kvs)
    scale = HD ** -0.5 * LOG2E
    tall = rows + 3 * pad_rows(rows)
    live = jnp.max(flags).reshape(1)
    listed = jnp.concatenate([flags.reshape(-1), live])
    here = pl.BlockSpec((rows, HD), lambda h: (0, h))
    key_part, value_part = kv_specs(kvs[0])
    operands = []
    for kv in kvs:
        operands += [kv, kv]
    return pl.pallas_call(
        functools.partial(far_kernel, slots, scale),
        grid=(heads,),
        in_specs=[pl.BlockSpec(memory_space=pltpu.SMEM), here] + [key_part, value_part] * slots,
        out_specs=pl.BlockSpec((tall, HD), lambda h: (0, h)),
        out_shape=jax.ShapeDtypeStruct((tall, width), jnp.bfloat16),
        scratch_shapes=[pltpu.VMEM((pad_rows(rows), BLOCK), jnp.float32)],
        cost_estimate=pl.CostEstimate(
            flops=4 * slots * rows * rows * width,
            bytes_accessed=2 * rows * width * (2 + 2 * slots),
            transcendentals=slots * rows * rows * heads,
        ),
        compiler_params=pltpu.CompilerParams(vmem_limit_bytes=40 << 20),
    )(listed, q, *operands)


def near_kernel(scale, has_ref, q_ref, k_ref, v_ref, far_ref, odd_ref, out_ref):
    rows = q_ref.shape[0]
    tile = tile_rows(rows)
    pad = pad_rows(rows)

    def log_sums(ref, has):
        pieces = [
            ref[rows + p * pad : rows + (p + 1) * pad, :].astype(jnp.float32) for p in range(3)
        ]
        return jnp.where(has, (pieces[0] + pieces[1]) + pieces[2], MASKED)

    far_all = log_sums(far_ref, has_ref[0] > 0)
    odd_all = log_sums(odd_ref, has_ref[1] > 0)
    wide = with_ones(flat(v_ref))
    head_keys = flat(k_ref)
    below = (
        lax.broadcasted_iota(jnp.int32, (tile, tile), 0)
        >= lax.broadcasted_iota(jnp.int32, (tile, tile), 1)
    )
    for index in range(rows // tile):
        start = index * tile
        end = start + tile
        q = q_ref[start:end, :]
        s = lax.dot_general(
            q, head_keys[0:end, :], (((1,), (1,)), ((), ())), preferred_element_type=jnp.float32
        ) * scale
        corner = jnp.where(below, s[:, start:end], MASKED)
        s = jnp.concatenate([s[:, :start], corner], axis=1) if index else corner
        top = jnp.max(s, axis=1, keepdims=True)
        e = jnp.exp2(s - top).astype(jnp.bfloat16)
        mix = jnp.dot(e, wide[0:end, :], preferred_element_type=jnp.float32)
        for r in range(start, end, BLOCK):
            part = slice(r - start, r - start + BLOCK)
            line = r // BLOCK
            far = as_rows(far_all[line : line + 1, :])
            odd = as_rows(odd_all[line : line + 1, :])
            best = jnp.maximum(jnp.maximum(far, odd), top[part])
            own_w = jnp.exp2(top[part] - best)
            far_w = jnp.exp2(far - best)
            odd_w = jnp.exp2(odd - best)
            numerator = (
                mix[part, :HD] * own_w
                + far_ref[r : r + BLOCK, :].astype(jnp.float32) * far_w
                + odd_ref[r : r + BLOCK, :].astype(jnp.float32) * odd_w
            )
            out_ref[r : r + BLOCK, :] = (
                numerator / (mix[part, HD:] * own_w + far_w + odd_w)
            ).astype(jnp.bfloat16)


def near_attention(has, q, kv, far, odd):
    rows, width = q.shape
    heads = width // HD
    scale = HD ** -0.5 * LOG2E
    here = pl.BlockSpec((rows, HD), lambda h: (0, h))
    key_part, value_part = kv_specs(kv)
    tall = pl.BlockSpec((far.shape[0], HD), lambda h: (0, h))
    return pl.pallas_call(
        functools.partial(near_kernel, scale),
        grid=(heads,),
        in_specs=[pl.BlockSpec(memory_space=pltpu.SMEM), here, key_part, value_part, tall, tall],
        out_specs=here,
        out_shape=jax.ShapeDtypeStruct((rows, width), jnp.bfloat16),
        cost_estimate=pl.CostEstimate(
            flops=2 * rows * rows * width,
            bytes_accessed=2 * rows * width * 6,
            transcendentals=rows * rows * heads // 2,
        ),
        compiler_params=pltpu.CompilerParams(vmem_limit_bytes=40 << 20),
    )(has, q, kv, kv, far, odd)


def body(queries, keys, values, pattern):
    groups = lax.axis_size("head")
    spans = lax.axis_size("ctx")
    position = lax.axis_index("ctx")
    far = spans // 2
    tok_rows, width = queries.shape
    rows = tok_rows * groups
    group_width = width // groups
    w = group_width // CHUNKS

    to_low = [(q, q - far) for q in range(far, spans)]
    to_high = [(b, a) for a, b in to_low]
    odd_low = [(far - 1, 0), (spans - 1, far)]
    odd_high = [(b, a) for a, b in odd_low]
    swap = [(c, c ^ 1) for c in range(far)]
    relay = [(c, c + 2) for c in range(0, far - 2, 2)] + [(c, c - 2) for c in range(3, far, 2)]

    move = lambda value, pairs: lax.ppermute(value, "ctx", pairs)

    own_flags = pattern[:, 0]
    low_flags = move(own_flags, to_low)
    odd_flags = move(own_flags[:1], odd_low)
    after = jnp.where(position == far - 1, 0, low_flags[0])
    before = jnp.where(position == 0, 0, low_flags[2])
    even = position % 2 == 0
    slot_flags = jnp.stack(
        [low_flags[1], jnp.where(even, after, before), jnp.where(even, before, after)]
    )
    has = jnp.stack(
        [position >= far, (position == far - 1) | (position == spans - 1)]
    ).astype(jnp.int32)

    def columns(array, group, chunk):
        first = group * group_width + chunk * w
        return lax.slice_in_dim(array, first, first + w, axis=1)

    def grouped(arrays, chunk):
        return jnp.concatenate(
            [
                columns(array, group, chunk)
                for group in range(groups)
                for array in arrays
            ],
            axis=0,
        ).reshape(groups, len(arrays) * tok_rows, w)

    def regroup(array):
        return lax.all_to_all(array, "head", split_axis=0, concat_axis=0, tiled=True)

    def gather(chunk, state):
        kv = regroup(grouped([state["keys"], state["values"]], chunk)).reshape(
            groups, 2, tok_rows, w
        )
        q = regroup(grouped([state["queries"]], chunk)).reshape(rows, w)
        return {"kv": kv, "q": q}

    def spread(item):
        return {
            **item,
            "q_low": move(item["q"], to_low),
            "q_odd": move(item["q"], odd_low),
            "kv_pair": move(item["kv"], swap),
        }

    def pass_on(item):
        return {
            **item,
            "kv_next": move(item["kv_pair"], relay),
            "odd_out": far_attention(state["odd_flags"], item["q_odd"], [item["kv"]]),
        }

    def attend(item):
        out = far_attention(
            state["slot_flags"], item["q_low"], [item["kv"], item["kv_pair"], item["kv_next"]]
        )
        return {
            "q": item["q"],
            "kv": item["kv"],
            "far_out": out,
            "odd_out": move(item["odd_out"], odd_high),
        }

    def give_back(item):
        return {
            **item,
            "far_out": move(item["far_out"], to_high),
        }

    def finish(item):
        mixed = near_attention(has, item["q"], item["kv"], item["far_out"], item["odd_out"])
        return {"done": regroup(mixed.reshape(groups, tok_rows, w))}

    stages = (spread, pass_on, attend, give_back, finish)
    state = {
        "queries": queries,
        "keys": keys,
        "values": values,
        "slot_flags": slot_flags,
        "odd_flags": odd_flags,
    }
    state = lax.optimization_barrier(state)
    items = {}
    for step in range(CHUNKS + len(stages)):
        ahead = {}
        for chunk in range(CHUNKS):
            stage = step - chunk
            if stage == 0:
                ahead[chunk] = gather(chunk, state)
            elif 0 < stage <= len(stages):
                ahead[chunk] = stages[stage - 1](items[chunk])
            elif chunk in items:
                ahead[chunk] = items[chunk]
        items, state = lax.optimization_barrier((ahead, state))
    results = [items[chunk]["done"] for chunk in range(CHUNKS)]
    return jnp.concatenate(
        [results[chunk][group] for group in range(groups) for chunk in range(CHUNKS)], axis=1
    )


def solution(mesh):
    rows = P(("ctx", "head"), None)
    return jax.shard_map(
        body,
        mesh=mesh,
        in_specs=(rows, rows, rows, P(None, "ctx", None, None)),
        out_specs=rows,
        check_vma=False,
    )
```
